32 devices in a mesh: rows: 16 (over z, y, x), ch: 2 (over core).
Axes of the slice: x: 2, y: 2, z: 4, core: 2. Of those that a mesh axis runs over, the one named last changes fastest.
Arguments:
- pixels: bfloat16 [32, 917504], P('ch', 'rows'), may hold values from -12 to 12
- skip_map: bfloat16 [64, 229376], P('ch', 'rows'), may hold values from -6 to 6
- style_map: bfloat16 [2048, 28, 256], P('rows'), may hold values from -12 to 12
- crop_rows: int32 [18], replicated, may hold values from 1 to 224, 2048 in all
- crop_group: int32 [18], replicated, may hold values from 0 to 3, as said below
- enc_first: bfloat16 [3, 3, 32, 64], P(None, None, None, 'ch'), may hold values from -0.375 to 0.375
- enc_convs: bfloat16 [3, 3, 3, 64, 64], P(None, None, None, None, 'ch'), may hold values from -0.25 to 0.25
- enc_skip: bfloat16 [32, 64], P(None, 'ch'), may hold values from -1 to 1
- enc_in_gain: float32 [2, 32], P(None, 'ch'), may hold values from 0.1 to 1.9
- enc_in_shift: float32 [2, 32], P(None, 'ch'), may hold values from -2.5 to 2.5
- enc_gain: float32 [3, 64], P(None, 'ch'), may hold values from 0.1 to 1.9
- enc_shift: float32 [3, 64], P(None, 'ch'), may hold values from -2.5 to 2.5
- dec_convs: bfloat16 [4, 3, 3, 64, 64], P(None, None, None, None, 'ch'), may hold values from -0.25 to 0.25
- dec_skip: bfloat16 [64, 64], P(None, 'ch'), may hold values from -0.75 to 0.75
- dec_gain: float32 [5, 64], P(None, 'ch'), may hold values from 0.1 to 1.9
- dec_shift: float32 [5, 64], P(None, 'ch'), may hold values from -2.5 to 2.5
- dense: bfloat16 [3, 256, 64], P(None, None, 'ch'), may hold values from -6 to 6
- out_grad: bfloat16 [64, 229376], P('ch', 'rows'), may hold values from -6 to 6
Outputs:
- decoded: float32 [64, 229376], P('ch', 'rows')
- pixels_grad: float32 [32, 917504], P('ch', 'rows')
- skip_grad: float32 [64, 229376], P('ch', 'rows')
- enc_first_grad: float32 [3, 3, 32, 64], P(None, None, None, 'ch')
- enc_convs_grad: float32 [3, 3, 3, 64, 64], P(None, None, None, None, 'ch')
- enc_skip_grad: float32 [32, 64], P(None, 'ch')
- enc_in_gain_grad: float32 [2, 32], P(None, 'ch')
- enc_in_shift_grad: float32 [2, 32], P(None, 'ch')
- enc_gain_grad: float32 [3, 64], P(None, 'ch')
- enc_shift_grad: float32 [3, 64], P(None, 'ch')
- dec_convs_grad: float32 [4, 3, 3, 64, 64], P(None, None, None, None, 'ch')
- dec_skip_grad: float32 [64, 64], P(None, 'ch')
- dec_gain_grad: float32 [5, 64], P(None, 'ch')
- dec_shift_grad: float32 [5, 64], P(None, 'ch')
- dense_grad: float32 [3, 256, 64], P(None, None, 'ch')
The draws below stay inside these ranges and needn't reach their ends.
Inputs may be any that keep to these rules, and one draw needn't show every extreme that they name: `crop_rows`: the crops lie one after another from row 0 and fill all 2048 pooled rows; the tallest has exactly 224 rows. `crop_group`: group 0 and group 3 each hold at least one crop; at least one group holds none.
All inputs are finite; a program needn't handle non-finite values.
Results may differ from the reference program's by a relative error of at most 0.025.
Values may be sent and summed in bfloat16 or wider, within the bound.
No kernel may reach another device: no remote copies, remote signals or barrier semaphores. Data moves between devices by JAX's collectives and lax.ppermute only.
A program may use at most 384 MiB of HBM per device.

```python
import math
import jax
import jax.numpy as jnp
import numpy as np
from jax import lax

C_IN = 32
C_MID = 64
STYLE_C = 256
FULL_W = 224
GROUPS = 4
POOL_W = 112
STYLE_W = 28
TOTAL_ROWS = 2048
CROPS = 18
CROP_MOST = 224


def row_factor(row_count):
    rising = jnp.arange(row_count, dtype=jnp.float32) / row_count - 0.5
    return jnp.exp(math.log(3.0) * rising)[:, None, None]


def draw_pixels(key, part):
    key = jax.random.fold_in(key, 11)
    array_shape = (2 * TOTAL_ROWS, FULL_W, C_IN)
    values = jnp.clip(jax.random.normal(key, array_shape, jnp.float32), -4.0, 4.0)
    scaled = values * row_factor(2 * TOTAL_ROWS)
    return jnp.transpose(scaled, (2, 0, 1)).reshape(C_IN, 2 * TOTAL_ROWS * FULL_W).astype(jnp.bfloat16)


def draw_style_map(key, part):
    key = jax.random.fold_in(key, 12)
    array_shape = (TOTAL_ROWS, STYLE_W, STYLE_C)
    values = jnp.clip(jax.random.normal(key, array_shape, jnp.float32), -4.0, 4.0)
    return (values * row_factor(TOTAL_ROWS)).astype(jnp.bfloat16)


def draw_crop_group(key, part):
    key = jax.random.fold_in(key, 13)
    empty_key, value_key, place_key = jax.random.split(key, 3)
    missing = jax.random.randint(empty_key, (), 1, GROUPS - 1, dtype=jnp.int32)
    values = jax.random.randint(value_key, (CROPS,), 0, GROUPS - 1, dtype=jnp.int32)
    values = values + (values >= missing).astype(jnp.int32)
    order = jax.random.permutation(place_key, CROPS)
    values = values.at[order[0]].set(0).at[order[1]].set(GROUPS - 1)
    return values.astype(jnp.int32)


def shard_levels(key, dims, cuts, least, top_value):
    gain, own = 1.0, jax.random.fold_in(key, 6)
    for position, parts in cuts:
        steps = jnp.exp(jax.random.uniform(jax.random.fold_in(own, position), (parts,), jnp.float32, least / len(cuts), top_value / len(cuts)))
        gain = gain * jnp.repeat(steps, dims[position] // parts).reshape([-1 if axis == position else 1 for axis in range(len(dims))])
    return gain


def length_profile(amount, total, most, slope):
    weights = [(1 << 20) // math.isqrt(grade ** slope) + 1 for grade in range(2, amount + 1)]
    surplus, counts = total - most - (amount - 1), [1] * (amount - 1)
    while surplus > 0:
        free = [i for i in range(amount - 1) if counts[i] < most]
        whole, budget = sum([weights[i] for i in free]), surplus
        for i in free:
            addition = min(most - counts[i], max(1, budget * weights[i] // whole), surplus)
            counts[i] = counts[i] + addition
            surplus = surplus - addition
    return np.array([most] + counts)


def uneven(own_key, amount, total, bound, slope):
    if amount == 2:
        one = jax.random.randint(own_key, (), max(1, total - bound), min(bound, total - 1) + 1)
        return jnp.stack([one, total - one])
    sizes = jnp.asarray(length_profile(amount, total, bound, slope), jnp.int32)
    twos = (amount - 1) // 2
    giver, receiver = sizes[1:1 + 2 * twos:2], sizes[2:2 + 2 * twos:2]
    slack = jnp.minimum(giver - 1, bound - receiver)
    passed = jax.random.randint(jax.random.fold_in(own_key, 1), (twos,), 0, 1 << 20) % (slack + 1)
    sizes = sizes.at[1:1 + 2 * twos:2].set(giver - passed).at[2:2 + 2 * twos:2].set(receiver + passed)
    return sizes[jax.random.permutation(jax.random.fold_in(own_key, 2), amount)]


def centred(own_key, dims, scale, reach, pieces=(), held_as=jnp.bfloat16):
    values = scale * jax.random.normal(own_key, dims, jnp.float32)
    if pieces:
        values = values * shard_levels(own_key, dims, pieces, -0.22, 0.18)
    return jnp.clip(values, -reach, reach).astype(held_as)


def setup_inputs(seed: int = 0) -> dict:
    key_of = jax.random.split(jax.random.key(seed), 19)
    return {
        "pixels": draw_pixels(jax.random.fold_in(key_of[18], 71), 0),
        "skip_map": centred(key_of[1], (C_MID, TOTAL_ROWS * POOL_W), 1.0, 6.0, ((0, 2), (1, 16))),
        "style_map": draw_style_map(jax.random.fold_in(key_of[18], 71), 0),
        "crop_rows": uneven(key_of[3], CROPS, TOTAL_ROWS, CROP_MOST, 0).astype(jnp.int32),
        "crop_group": draw_crop_group(jax.random.fold_in(key_of[18], 71), 0),
        "enc_first": centred(key_of[5], (3, 3, C_IN, C_MID), (9 * C_IN) ** -0.5, 0.375, ((3, 2),)),
        "enc_convs": centred(key_of[6], (3, 3, 3, C_MID, C_MID), (9 * C_MID) ** -0.5, 0.25, ((4, 2),)),
        "enc_skip": centred(key_of[7], (C_IN, C_MID), C_IN ** -0.5, 1.0, ((1, 2),)),
        "enc_in_gain": jnp.clip(1.0 + 0.18 * jax.random.normal(key_of[8], (2, C_IN), jnp.float32), 0.1, 1.9),
        "enc_in_shift": centred(key_of[9], (2, C_IN), 0.3, 2.5, ((1, 2),), jnp.float32),
        "enc_gain": jnp.clip(1.0 + 0.18 * jax.random.normal(key_of[10], (3, C_MID), jnp.float32), 0.1, 1.9),
        "enc_shift": centred(key_of[11], (3, C_MID), 0.3, 2.5, ((1, 2),), jnp.float32),
        "dec_convs": centred(key_of[12], (4, 3, 3, C_MID, C_MID), (9 * C_MID) ** -0.5, 0.25, ((4, 2),)),
        "dec_skip": centred(key_of[13], (C_MID, C_MID), C_MID ** -0.5, 0.75, ((1, 2),)),
        "dec_gain": jnp.clip(1.0 + 0.18 * jax.random.normal(key_of[14], (5, C_MID), jnp.float32), 0.1, 1.9),
        "dec_shift": centred(key_of[15], (5, C_MID), 0.3, 2.5, ((1, 2),), jnp.float32),
        "dense": centred(key_of[16], (3, STYLE_C, C_MID), 1 ** -0.5, 6.0, ((2, 2),)),
        "out_grad": centred(key_of[17], (C_MID, TOTAL_ROWS * POOL_W), 1.0, 6.0, ((0, 2), (1, 16))),
    }


epsilon = 1e-05
precise = lax.Precision.HIGHEST

@jax.custom_vjp
def low(v):
    return lax.optimization_barrier(v.astype(jnp.bfloat16)).astype(jnp.float32)

@jax.custom_vjp
def low_back(v):
    return v

def low_keep(v):
    return (low(v), None)

def low_pass(kept, grad):
    return (grad,)

def back_keep(v):
    return (v, None)

def back_low(kept, grad):
    return (low(grad),)
low.defvjp(low_keep, low_pass)
low_back.defvjp(back_keep, back_low)

def to_maps(flat, width):
    return jnp.transpose(flat.reshape(flat.shape[0], -1, width), (1, 2, 0))

def from_maps(maps):
    return jnp.transpose(maps, (2, 0, 1)).reshape(maps.shape[2], -1)

def crop_of(row_ids, crop_ends):
    return lax.optimization_barrier(jnp.sum((row_ids[:, None] >= crop_ends[None, :]).astype(jnp.int32), axis=1))

def pool_pixels(pixels_f):
    row_total, full_width, channels = pixels_f.shape
    return lax.optimization_barrier(jnp.mean(pixels_f.reshape(row_total // 2, 2, full_width // 2, 2, channels), axis=(1, 3)))

def batch_norm(values, norm_gain, norm_shift):
    center = lax.optimization_barrier(jnp.mean(values, axis=(0, 1)))
    variance = lax.optimization_barrier(jnp.mean(values * values, axis=(0, 1))) - center * center
    return (values - center) * lax.rsqrt(variance + epsilon) * norm_gain + norm_shift

def conv_three(inputs, kernel, up_keep, down_keep):
    pool_width = inputs.shape[1]
    zero_row = jnp.zeros((1,) + inputs.shape[1:], jnp.float32)
    above = jnp.concatenate([zero_row, inputs[:-1]], axis=0) * up_keep[:, None, None]
    below = jnp.concatenate([inputs[1:], zero_row], axis=0) * down_keep[:, None, None]
    result = jnp.zeros(inputs.shape[:2] + (kernel.shape[3],), jnp.float32)
    for row_tap, source in enumerate((above, inputs, below)):
        padded = jnp.pad(source, ((0, 0), (1, 1), (0, 0)))
        for col_tap in range(3):
            result = result + jnp.einsum('rwc,cd->rwd', padded[:, col_tap:col_tap + pool_width], kernel[row_tap, col_tap], precision=precise)
    return result

def skip_conv(inputs, kernel):
    return jnp.einsum('rwc,cd->rwd', inputs, kernel, precision=precise)

def reference(pixels, skip_map, style_map, crop_rows, crop_group, enc_first, enc_convs, enc_skip, enc_in_gain, enc_in_shift, enc_gain, enc_shift, dec_convs, dec_skip, dec_gain, dec_shift, dense, out_grad):
    crop_ends = jnp.cumsum(crop_rows).astype(jnp.int32)
    crop_ids = crop_of(jnp.arange(TOTAL_ROWS, dtype=jnp.int32), crop_ends)
    joined = (crop_ids[1:] == crop_ids[:-1]).astype(jnp.float32)
    border = jnp.zeros((1,), jnp.float32)
    up_keep = jnp.concatenate([border, joined])
    down_keep = jnp.concatenate([joined, border])
    member_rows = (crop_ids[:, None] == jnp.arange(CROPS, dtype=jnp.int32)[None, :]).astype(jnp.float32)
    crop_totals = jnp.dot(member_rows.T, lax.optimization_barrier(jnp.sum(style_map.astype(jnp.float32), axis=1)), precision=precise)
    group_member = (crop_group[:, None] == jnp.arange(GROUPS, dtype=jnp.int32)[None, :]).astype(jnp.float32)
    group_totals = jnp.dot(group_member.T, crop_totals, precision=precise)
    group_pixels = jnp.dot(group_member.T, crop_rows.astype(jnp.float32) * STYLE_W, precision=precise)
    group_means = group_totals / jnp.maximum(group_pixels, 1.0)[:, None]
    group_unit = group_means * lax.rsqrt(lax.optimization_barrier(jnp.sum(group_means * group_means, axis=1, keepdims=True)) + 1e-06)
    crop_style = jnp.dot(group_member, group_unit, precision=precise)

    def conv(inputs, kernel):
        return conv_three(inputs, kernel, up_keep, down_keep)

    def forward(pixels_f, skip_f, first_f, econv_f, eskip_f, ein_gain, ein_shift, egain_f, eshift_f, dconv_f, dskip_f, dgain_f, dshift_f, dense_f):
        feature_rows = [jnp.dot(member_rows, jnp.dot(crop_style, dense_f[layer], precision=precise), precision=precise)[:, None, :] for layer in range(3)]
        pooled = pool_pixels(pixels_f)
        act_a0 = low(jax.nn.gelu(batch_norm(pooled, ein_gain[1], ein_shift[1])))
        normed_s0 = low(batch_norm(pooled, ein_gain[0], ein_shift[0]))
        hidden_h0 = low_back(conv(act_a0, first_f))
        act_a1 = low(jax.nn.gelu(batch_norm(hidden_h0, egain_f[0], eshift_f[0])))
        section_e1 = low_back(skip_conv(normed_s0, eskip_f)) + low_back(conv(act_a1, econv_f[0]))
        act_a2 = low(jax.nn.gelu(batch_norm(section_e1, egain_f[1], eshift_f[1])))
        hidden_h2 = low_back(conv(act_a2, econv_f[1]))
        act_a3 = low(jax.nn.gelu(batch_norm(hidden_h2, egain_f[2], eshift_f[2])))
        section_e2 = section_e1 + low_back(conv(act_a3, econv_f[2]))
        act_b0 = low(jax.nn.gelu(batch_norm(section_e2, dgain_f[1], dshift_f[1])))
        normed_q0 = low(batch_norm(section_e2, dgain_f[0], dshift_f[0]))
        section_u1 = low_back(conv(act_b0, dconv_f[0])) + skip_f + feature_rows[0]
        act_b1 = low(jax.nn.gelu(batch_norm(section_u1, dgain_f[2], dshift_f[2])))
        section_d1 = low_back(skip_conv(normed_q0, dskip_f)) + low_back(conv(act_b1, dconv_f[1]))
        section_u2 = section_d1 + skip_f + feature_rows[1]
        act_b2 = low(jax.nn.gelu(batch_norm(section_u2, dgain_f[3], dshift_f[3])))
        section_u3 = low_back(conv(act_b2, dconv_f[2])) + feature_rows[2]
        act_b3 = low(jax.nn.gelu(batch_norm(section_u3, dgain_f[4], dshift_f[4])))
        return section_d1 + low_back(conv(act_b3, dconv_f[3]))
    pixel_maps = to_maps(pixels.astype(jnp.float32), FULL_W)
    skip_maps = to_maps(skip_map.astype(jnp.float32), POOL_W)
    floats = (pixel_maps, skip_maps, enc_first.astype(jnp.float32), enc_convs.astype(jnp.float32), enc_skip.astype(jnp.float32), enc_in_gain.astype(jnp.float32), enc_in_shift.astype(jnp.float32), enc_gain.astype(jnp.float32), enc_shift.astype(jnp.float32), dec_convs.astype(jnp.float32), dec_skip.astype(jnp.float32), dec_gain.astype(jnp.float32), dec_shift.astype(jnp.float32), dense.astype(jnp.float32))
    decoded, pullback = jax.vjp(forward, *floats)
    grads = pullback(to_maps(out_grad.astype(jnp.float32), POOL_W))
    return (from_maps(decoded), from_maps(grads[0]), from_maps(grads[1]), grads[2], grads[3], grads[4], grads[5], grads[6], grads[7], grads[8], grads[9], grads[10], grads[11], grads[12], grads[13])
```

```python
import functools

import jax
import jax.numpy as jnp
from jax import lax
from jax.experimental import pallas as pl
from jax.experimental.pallas import tpu as pltpu
from jax.sharding import PartitionSpec as P

FULL_W = 224
GROUPS = 4
POOL_W = 112
LANES = 128
HALO = 14
STEP_AHEAD = 32
STEP_BACK = 24

epsilon = 1e-05
gelu_scale = 0.7978845608
gelu_cubic = 0.7978845608 * 0.044715

both = ("rows", "ch")
f32 = jnp.float32
bf16 = jnp.bfloat16

VMEM = pl.BlockSpec(memory_space=pltpu.VMEM)
SMEM = pl.BlockSpec(memory_space=pltpu.SMEM)


def call(kernel, name, ins, outs, scratch=(), limit=5, cost=4, after=()):
    count = len(ins)

    def body(*refs):
        kernel(*refs[:count], *refs[count + len(after) :])

    spaces = {True: SMEM, False: VMEM, "hbm": pl.BlockSpec(memory_space=pltpu.HBM)}
    in_specs = [spaces[kind] for _, kind in ins]
    in_specs += [pl.BlockSpec(memory_space=pl.ANY)] * len(after)
    return pl.pallas_call(
        body,
        name=name,
        out_shape=tuple(jax.ShapeDtypeStruct(out[0], out[1]) for out in outs),
        in_specs=in_specs,
        out_specs=tuple(spaces[out[2] if len(out) > 2 else False] for out in outs),
        scratch_shapes=list(scratch),
        compiler_params=pltpu.CompilerParams(vmem_limit_bytes=limit * 2**20),
        cost_estimate=pl.CostEstimate(
            flops=0, bytes_accessed=int(cost * 3_500_000), transcendentals=0
        ),
    )(*[value for value, _ in ins], *after)


def lanes_of(shape):
    return lax.broadcasted_iota(jnp.int32, shape, len(shape) - 1)


def roll(tile, amount):
    return pltpu.roll(tile, amount % LANES, axis=1)


def dot(lhs, rhs):
    return jnp.dot(lhs, rhs, preferred_element_type=f32)


def gelu(half):
    inner = jnp.tanh(half * (2.0 * gelu_scale + (8.0 * gelu_cubic) * (half * half)))
    return half + half * inner


def gelu_slope(half):
    square = half * half
    inner = jnp.tanh(half * (2.0 * gelu_scale + (8.0 * gelu_cubic) * square))
    slope = gelu_scale + (12.0 * gelu_cubic) * square
    return (0.5 + 0.5 * inner) + (half * slope) * (1.0 - inner * inner)


def total_of(stats, slot, period=1):
    total = None
    for part in stats:
        values = part[:, :LANES]
        if period > 1:
            rows = lax.broadcasted_iota(jnp.int32, values.shape, 0)
            values = jnp.where(rows % period == slot, values, 0.0)
        values = jnp.sum(values, axis=0, keepdims=True)
        total = values if total is None else total + values
    return total


def take(refs, count):
    return [refs.pop(0) for _ in range(count)]


def columns_of(stats, slot, period=1):
    total = total_of(stats, slot, period)
    return jnp.transpose(jnp.broadcast_to(total, (LANES, LANES)))


def row_of(*parts):
    tall = jnp.concatenate(parts, axis=0)
    return jnp.sum(jnp.transpose(tall), axis=0, keepdims=True)


def settle(stats, channels, inv_count):
    columns = columns_of(stats, 0)
    center = columns[:channels] * inv_count
    variance = columns[channels : 2 * channels] * inv_count - center * center
    return center, lax.rsqrt(variance + epsilon)


def affine(center, scale, norm):
    gain = scale * norm[0]
    return gain, norm[1] - center * gain


def halved(columns):
    return [0.5 * value for value in columns]


def inner_only(*columns):
    return [jnp.where(lanes_of(value.shape) < POOL_W, value, 0.0) for value in columns]


def back_columns(sums, slot, channels, first, center, scale, gain, inv_count, period=1):
    columns = columns_of(sums, slot, period)
    shift_sum = columns[first : first + channels] * inv_count
    gain_sum = columns[first + channels : first + 2 * channels] * inv_count
    outer = gain * scale
    slope = outer * scale * gain_sum
    return outer, slope, center * slope - outer * shift_sum


def three_wide(tile):
    low = tile.astype(bf16)
    return [roll(low, 1), low, roll(low, -1)]


def conv_rows(first, count, weights, width, keep, held, produce, emit, extra=None, weigh=None):
    held[...] = jnp.zeros_like(held)

    def chunk(row, height):
        products = []
        sources = []
        for pair in range(height // 2):
            source = jnp.concatenate(
                [jnp.concatenate(produce(row + 2 * pair + k), axis=0) for k in range(2)], axis=1
            )
            products.append(dot(weights(), source))
            sources.append(source)
        if weigh is not None:
            for start in range(0, height, 16):
                size = min(16, height - start)
                weigh(row + start, size, sources[start // 2 : (start + size) // 2])

        def block(group, k):
            lanes = slice(LANES * (k % 2), LANES * (k % 2 + 1))
            return products[k // 2][group * width : (group + 1) * width, lanes]

        links = [keep[0, row + k].astype(f32) for k in range(height)]
        rows = [held[1] + links[0] * block(2, 0)]
        for k in range(height - 1):
            above = held[0] if k == 0 else block(0, k - 1)
            rows.append(links[k] * above + block(1, k) + links[k + 1] * block(2, k + 1))
        last = block(1, height - 1) + links[height - 1] * block(0, height - 2)
        held[0] = block(0, height - 1)
        held[1] = last
        if extra is not None:
            for k in range(height):
                lanes = slice(LANES * (k % 2), LANES * (k % 2 + 1))
                extra(row + k, products[k // 2][3 * width :, lanes])
        emit(row - 1, rows)

    height = STEP_AHEAD if weigh is None else STEP_BACK

    def body(step, carry):
        chunk(first + height * step, height)
        return carry

    steps = count // height
    lax.fori_loop(0, steps, body, 0)
    if count % height:
        chunk(first + height * steps, count % height)


def own_place(row, own_rows):
    return jnp.clip(row - HALO, -2, own_rows + 1) + 2


def own_limit(row, own_rows):
    inside = jnp.logical_and(row >= HALO, row < HALO + own_rows)
    return jnp.where(inside, POOL_W, 0)


def add_stats(acc, row, first_values, second_values, own_rows):
    lanes = lanes_of(first_values[0].shape)
    one = None
    two = None
    for k, (left, right) in enumerate(zip(first_values, second_values)):
        kept = jnp.where(lanes < own_limit(row + k, own_rows), left, 0.0)
        other = kept * right
        one = kept if one is None else one + kept
        two = other if two is None else two + other
    acc[0] += one
    acc[1] += two


def forward_kernel(
    spec, own_rows, inv_count, *refs
):
    (f, cin, cout, has_skip_in, side_norm, features, keep_raw, layer, spots, seen) = spec
    refs = list(refs)
    keep = refs.pop(0)
    values = refs.pop(0)
    stats = take(refs, seen)
    norms = refs.pop(0)
    norm, side = norms.at[spots[0]], norms.at[spots[-1]]
    weight_stack = refs.pop(0)
    depth = 3 * cin + (0 if not has_skip_in else 32 if layer == 1 else 64)

    def weights():
        return weight_stack[layer, :, :depth]

    skip_in = refs.pop(0) if has_skip_in else None
    residual = refs.pop(0) if "residual" in features else None
    skip_map = refs.pop(0) if "skip" in features else None
    feature = refs.pop(0) if "feature" in features else None
    payload = refs.pop(0) if "payload" in features else None
    result = refs.pop(0)
    raw = refs.pop(0) if keep_raw else None
    act = refs.pop(0)
    side_out = refs.pop(0) if side_norm else None
    columns_out = refs.pop(0)
    stats_out = refs.pop(0)
    held = refs.pop(0)
    acc = refs.pop(0)
    acc[...] = jnp.zeros_like(acc)
    center, scale = settle(stats, cin, inv_count)
    columns_out[0] = center
    columns_out[1] = scale
    gain, shift = inner_only(*halved(affine(center, scale, norm)))
    if side_norm:
        side_gain, side_shift = inner_only(*affine(center, scale, side))

    def produce(row):
        value = values[row]
        active = gelu(value * gain + shift)
        pieces = three_wide(active)
        act[own_place(row, own_rows)] = pieces[1]
        if side_norm:
            side_out[row] = (value * side_gain + side_shift).astype(bf16)
        if has_skip_in:
            pieces.append(skip_in[row])
        return pieces

    def emit(row, rows):
        if residual is not None:
            rows = [value + residual[row + k] for k, value in enumerate(rows)]
        if raw is not None:
            for k, value in enumerate(rows):
                raw[own_place(row + k, own_rows)] = value
        if skip_map is not None:
            rows = [value + skip_map[row + k].astype(f32) for k, value in enumerate(rows)]
        if feature is not None:
            turned = pltpu.roll(feature[...], LANES - jnp.maximum(row, 0), axis=1)
            rows = [
                value + jnp.broadcast_to(turned[:, k : k + 1], (cout, LANES))
                for k, value in enumerate(rows)
            ]
        for k, value in enumerate(rows):
            result[jnp.maximum(row + k, 0)] = value
        add_stats(acc, row, rows, rows, own_rows)

    conv_rows(
        HALO - f - 1, own_rows + 2 * f + 2, weights, cout, keep, held, produce, emit
    )
    total = row_of(acc[0], acc[1])
    if payload is not None:
        total = jnp.concatenate([total, payload[...]], axis=1)
    stats_out[...] = jnp.broadcast_to(total, stats_out.shape)


def forward(name, keep, values, stats, norms, spots, weights, layer, f, own_rows, inv_count,
            out_rows, skip_in=None, residual=None, skip_map=None, feature=None, payload=None,
            keep_raw=False, after=()):
    total = own_rows + 2 * HALO
    cin = values.shape[1]
    cout = 64
    features = ()
    outs = []
    side = len(spots) > 1
    ins = [(keep, True), (values, False)]
    ins += [(part, False) for part in stats]
    ins += [(norms, False), (weights, False)]
    if skip_in is not None:
        ins.append((skip_in, False))
    if residual is not None:
        ins.append((residual, False))
        features += ("residual",)
    if skip_map is not None:
        ins.append((skip_map, False))
        features += ("skip",)
    if feature is not None:
        ins.append((feature, False))
        features += ("feature",)
    wide = LANES
    if payload is not None:
        ins.append((payload, False))
        features += ("payload",)
        wide += payload.shape[1]
    outs.append(((total, cout, LANES), f32))
    if keep_raw:
        outs.append(((own_rows + 4, cout, LANES), f32))
    outs.append(((own_rows + 4, cin, LANES), bf16))
    if side:
        outs.append(((total, cin, LANES), bf16))
    outs.append(((2, cin, LANES), f32))
    outs.append(((out_rows, wide), f32))
    spec = (f, cin, cout, skip_in is not None, side, features, keep_raw, layer, spots, len(stats))
    scratch = [pltpu.VMEM((2, cout, LANES), f32), pltpu.VMEM((2, cout, LANES), f32)]
    return call(
        functools.partial(forward_kernel, spec, own_rows, inv_count), name, ins, outs, scratch,
        after=after,
    )


def spread_lines(lines, period, out):
    rows = lax.broadcasted_iota(jnp.int32, out.shape, 0) % period
    value = jnp.zeros(out.shape, f32)
    for k, line in enumerate(lines):
        value = jnp.where(rows == k, jnp.broadcast_to(line, out.shape), value)
    out[...] = value


def group_lines(top, u3, d1, u1):
    lines = []
    for sums in (u1[...], d1[...] - top[...], u3[...]):
        for pair in range(GROUPS // 2):
            left = pltpu.roll(sums[2 * pair : 2 * pair + 1], 64, axis=1)
            right = sums[2 * pair + 1 : 2 * pair + 2]
            lines.append(jnp.where(lanes_of((1, LANES)) < 64, left, right))
    return lines


def decode_kernel(own_rows, keep, core, act, weight_stack, raw, kept, sent, held):
    first = core[0] == 0

    def weights():
        return weight_stack[7, :, :192]

    def produce(row):
        return three_wide(act[own_place(row, own_rows)])

    def emit(row, rows):
        for k, value in enumerate(rows):
            place = own_place(row + k, own_rows)
            value = (value + raw[place]).astype(bf16)
            low, high = value[:32], value[32:]
            kept[place] = jnp.where(first, low, high)
            sent[place] = jnp.where(first, high, low)

    conv_rows(HALO - 1, own_rows + 2, weights, 64, keep, held, produce, emit)


def backward_kernel(spec, own_rows, inv_count, *refs):
    (b, cout, cin, slopes_in, extra_in, below_sides, extra_rows, save, split, skip_rows, export,
     gathers, layer, spots, below_spot, seen) = spec
    refs = list(refs)
    keep = refs.pop(0)
    core = refs.pop(0)
    slopes = [refs.pop(0) for _ in range(slopes_in)]
    if slopes_in:
        values = refs.pop(0)
        columns = refs.pop(0)
        sums = take(refs, seen)
        norm_stack = refs.pop(0)
    norms = [norm_stack.at[spot] for spot in spots]
    extra = refs.pop(0) if extra_in else None
    weight_stack = refs.pop(0)

    def weights():
        return weight_stack[layer, : 3 * cin + extra_rows, :]

    below = refs.pop(0)
    below_columns = refs.pop(0)
    below_norm = refs.pop(0).at[below_spot]
    below_side = refs.pop(0) if below_sides else None
    other = refs.pop(0) if split else None
    act = refs.pop(0) if slopes_in else None
    skip_in = refs.pop(0) if skip_rows else None
    gathered = [refs.pop(0) for _ in range(gathers)]
    pure_out = refs.pop(0) if save else None
    slope_out = refs.pop(0)
    skip_out = refs.pop(0) if extra_rows else None
    kept = refs.pop(0) if split else None
    sent = refs.pop(0) if split else None
    stats_out = refs.pop(0)
    weights_kept = refs.pop(0)
    weights_sent = refs.pop(0)
    groups_out = refs.pop(0) if export else None
    if not slopes_in:
        act = refs.pop(0)
        columns_out = refs.pop(0)
        columns_out[0], columns_out[1] = settle([below_columns], cin, inv_count)
        below_columns = columns_out
    held = refs.pop(0)
    acc = refs.pop(0)
    total = refs.pop(0)
    acc[...] = jnp.zeros_like(acc)
    total[...] = jnp.zeros_like(total)
    first = core[0] == 0
    outers = []
    slope_col = None
    const_col = None
    if slopes_in:
        center, scale = columns[0], columns[1]
    for k, norm in enumerate(norms):
        outer, slope, const = back_columns(
            sums, k, cout, 0, center, scale, norm[0], inv_count, slopes_in
        )
        outers.append(outer)
        slope_col = slope if slope_col is None else slope_col + slope
        const_col = const if const_col is None else const_col + const
    gain, shift = halved(affine(below_columns[0], below_columns[1], below_norm))
    if slopes_in:
        slope_col, const_col, *outers = inner_only(slope_col, const_col, *outers)
    member_rows = lax.broadcasted_iota(jnp.int32, (16, LANES), 0)
    height = 3 * cin + skip_rows + (16 if export else 0)
    if not slopes_in:
        inner_gain, inner_shift = inner_only(gain, shift)

        def active(step, carry):
            for k in range(6):
                row = HALO - 1 + 6 * step + k
                act[6 * step + k + 1] = gelu(below[row] * inner_gain + inner_shift).astype(bf16)
            return carry

        lax.fori_loop(0, (own_rows + 2) // 6, active, 0)
        for row in range((own_rows + 2) // 6 * 6, own_rows + 2):
            act[row + 1] = gelu(below[HALO - 1 + row] * inner_gain + inner_shift).astype(bf16)

    def produce(row):
        if not slopes_in:
            return three_wide(extra[row])
        grad = const_col - values[row] * slope_col
        for slope, outer in zip(slopes, outers):
            grad = grad + slope[row] * outer
        place = own_place(row, own_rows)
        if save:
            pure_out[place if save == "own" else row] = grad
        if split:
            both_grads = grad + other[place]
            both_grads = both_grads.astype(bf16)
            low, high = both_grads[:32], both_grads[32:]
            kept[place] = jnp.where(first, low, high)
            sent[place] = jnp.where(first, high, low)
        if extra is not None:
            grad = grad + extra[row].astype(f32)
        return three_wide(grad)

    def emit(row, rows):
        results = []
        centred = []
        for k, value in enumerate(rows):
            lower = below[row + k]
            half = lower * gain + shift
            slope = gelu_slope(half) * value
            slope_out[own_place(row + k, own_rows) if cin == 32 else row + k] = slope
            results.append(slope)
            centred.append(half)
        add_stats(acc, row, results, centred, own_rows)
        if below_side is not None:
            sides = [
                below_side[own_place(row + k, own_rows) if cin == 32 else row + k]
                for k in range(len(rows))
            ]
            add_stats(acc.at[2:4], row, sides, centred, own_rows)

    def extra_emit(row, value):
        skip_out[own_place(row, own_rows) if extra_rows == 32 else row] = value

    def weigh(row, count, sources):
        lefts = []
        empty = jnp.zeros((cin, LANES), bf16)
        for k in range(count):
            at = row + k
            inside = jnp.logical_and(at >= HALO, at < HALO + own_rows)
            up = jnp.logical_and(inside, keep[0, at] > 0)
            down = jnp.logical_and(inside, keep[0, at + 1] > 0)
            place = jnp.clip(at - HALO, 0, own_rows - 1)
            left = [
                jnp.where(up, act[place + 1], empty),
                jnp.where(inside, act[place + 2], empty),
                jnp.where(down, act[place + 3], empty),
            ]
            if skip_rows:
                left.append(
                    jnp.where(inside, skip_in[at], jnp.zeros((skip_rows, LANES), bf16))
                )
            if export:
                group = jnp.where(inside, keep[1, at], -1)
                left.append((member_rows == group).astype(f32).astype(bf16))
            lefts.append(jnp.concatenate(left, axis=0))
        total[:height, :192] += lax.dot_general(
            jnp.concatenate(lefts, axis=1),
            jnp.concatenate(sources, axis=1),
            NT,
            preferred_element_type=f32,
        )

    conv_rows(
        HALO - b, own_rows + 2 * b, weights, cin, keep, held, produce, emit,
        extra_emit if extra_rows else None, weigh,
    )
    per_gain = 1.0 / below_norm[0]

    def by_unit(plain, halves):
        return (2.0 * halves - below_norm[1] * plain) * per_gain

    one = [acc[0], by_unit(acc[0], acc[1])]
    if below_side is not None:
        two = [acc[2], by_unit(acc[2], acc[3])]
        if cin == 32:
            spread_lines([row_of(*two, *one)] + group_lines(*gathered), 8, stats_out)
        else:
            spread_lines([row_of(*two), row_of(*one)], 2, stats_out)
    else:
        stats_out[...] = jnp.broadcast_to(row_of(*one), stats_out.shape)
    if export:
        groups_out[...] = total[3 * cin + skip_rows : 3 * cin + skip_rows + 8, :LANES]
    for start in range(0, weights_kept.shape[1], LANES):
        tall = total[start : start + LANES]
        turned = [jnp.transpose(tall[:, :LANES]), jnp.transpose(tall[:, LANES:])]
        taps = [turned[1][:64], turned[0][64:], turned[0][:64]]
        low = jnp.concatenate([tap[:32] for tap in taps], axis=0)
        high = jnp.concatenate([tap[32:] for tap in taps], axis=0)
        weights_kept[:, start : start + LANES] = jnp.where(first, low, high)
        weights_sent[:, start : start + LANES] = jnp.where(first, high, low)


def backward(name, keep, core, slopes, values, stats, sums, norms, spots, weights, layer, below,
             below_stats, below_norms, below_spot, act, b, own_rows, inv_count, out_rows,
             extra=None, below_side=None, extra_rows=0, save=False, other=None, skip_in=None,
             after=(), export=False, gathered=()):
    total = own_rows + 2 * HALO
    cout = 64
    cin = below.shape[1]
    ins = [(keep, True), (core, True)]
    split = other is not None
    ins += [(slope, False) for slope in slopes]
    if slopes:
        ins.append((values, False))
        ins.append((stats, False))
        ins += [(part, False) for part in sums]
        ins.append((norms, False))
    if extra is not None:
        ins.append((extra, False))
    ins += [(weights, False), (below, False)]
    ins += [(below_stats, False), (below_norms, False)]
    if below_side is not None:
        ins.append((below_side, False))
    if split:
        ins.append((other, False))
    if slopes:
        ins.append((act, False))
    if skip_in is not None:
        ins.append((skip_in, False))
    ins += [(value, False) for value in gathered]
    outs = []
    if save:
        outs.append(((own_rows + 4 if save == "own" else total, cout, LANES), f32))
    outs.append(((own_rows + 4 if cin == 32 else total, cin, LANES), f32))
    if extra_rows:
        outs.append(((own_rows + 4 if extra_rows == 32 else total, extra_rows, LANES), f32))
    if split:
        outs.append(((own_rows + 4, 32, LANES), bf16))
        outs.append(((own_rows + 4, 32, LANES), bf16))
    tall = out_rows if below_side is None else 2 * out_rows if cin == 64 else 8
    outs.append(((tall, LANES), f32))
    skip_rows = 0 if skip_in is None else skip_in.shape[1]
    height = -(-(3 * cin + skip_rows + 16) // LANES) * LANES
    width = -(-(3 * cin + skip_rows) // LANES) * LANES
    outs += [((96, width), f32), ((96, width), f32)]
    if export:
        outs.append(((8, LANES), f32))
    if not slopes:
        outs.append(((own_rows + 4, cin, LANES), bf16))
        outs.append(((2, cin, LANES), f32))
    spec = (b, cout, cin, len(slopes), extra is not None, below_side is not None, extra_rows,
            save, split, skip_rows, export, len(gathered), layer, spots, below_spot,
            len(sums))
    scratch = [
        pltpu.VMEM((2, cin, LANES), f32), pltpu.VMEM((4, cin, LANES), f32),
        pltpu.VMEM((height, 256), f32),
    ]
    return call(
        functools.partial(backward_kernel, spec, own_rows, inv_count), name, ins, outs, scratch,
        after=after,
    )


SKIP_HALO = 9
TOP_HALO = 8


def entry_kernel(own_rows, core, skip_in, top_in, pixels_in, mine, send_pair, send_same,
                 send_cross, stats_out, acc, skip, top, pixels, pool, maps, pooled_maps, arrived,
                 left):
    strip = 2 * own_rows
    pair_rows = own_rows + HALO
    first = core[0] == 0
    loads = [
        pltpu.make_async_copy(source, target, arrived.at[k])
        for k, (source, target) in enumerate(
            ((skip_in, skip), (top_in, top), (pixels_in, pixels))
        )
    ]
    for load in loads:
        load.start()
    home = pixel_home(lax.broadcasted_iota(jnp.int32, pool.shape, 0))
    pool[...] = jnp.where(home == lanes_of(pool.shape), 0.25, 0.0).astype(bf16)
    acc[...] = jnp.zeros_like(acc)
    wide = 4 * FULL_W
    other = 1 - core[0]
    stores = []

    def send(source, target):
        stores.append(pltpu.make_async_copy(source, target, left.at[len(stores)]))
        stores[-1].start()

    def send_part(local, channels, halos):
        for side, out in ((core[0], mine), (other, send_pair)):
            rows = pl.ds(side * (strip - pair_rows), pair_rows)
            send(local.at[rows], out.at[:, channels])
        for channel, count, at in halos:
            for side, out in ((other, send_same), (core[0], send_cross)):
                rows = pl.ds(side * (strip - count), count)
                send(local.at[rows, channel : channel + 32], out.at[at : at + count])

    loads[0].wait()
    loads[1].wait()
    lanes = lanes_of((32, LANES)).astype(f32).astype(bf16)
    zero = jnp.zeros((32, LANES), bf16)

    def body(step, carry):
        start = pl.multiple_of(step * 8 * POOL_W, LANES)
        for place, source in enumerate((skip, top)):
            flat = source[:, pl.ds(start, 8 * POOL_W)]
            tiles = [flat[:, LANES * k : LANES * (k + 1)] for k in range(7)]
            for k in range(8):
                if k == 0:
                    line = tiles[0]
                elif k == 7:
                    line = roll(tiles[6], 16 * 7)
                else:
                    line = jnp.where(
                        lanes < 16 * k, roll(tiles[k - 1], 16 * k), roll(tiles[k], 16 * k)
                    )
                line = jnp.where(lanes < POOL_W, line, zero)
                maps[8 * step + k, 32 * place : 32 * (place + 1)] = line
        return carry

    lax.fori_loop(0, strip // 8, body, 0)
    send_part(maps, slice(0, 64), ((0, SKIP_HALO, 0), (32, TOP_HALO, SKIP_HALO)))
    loads[2].wait()

    def pool_body(step, carry):
        source = jnp.concatenate(
            [
                pixels[:, pl.ds(pl.multiple_of((8 * step + k) * wide, LANES), wide)]
                for k in range(8)
            ],
            axis=0,
        )
        pooled = dot(source, pool[...])
        one = jnp.zeros((16, LANES), f32)
        two = jnp.zeros((16, LANES), f32)
        for k in range(8):
            for side in range(2):
                value = pooled[16 * k : 16 * (k + 1), LANES * side : LANES * (side + 1)]
                row = 16 * step + 2 * k + side
                upper = value.astype(bf16)
                pooled_maps[row, :16] = upper
                pooled_maps[row, 16:] = (value - upper.astype(f32)).astype(bf16)
                one = one + value
                two = two + value * value
        acc[0] += one
        acc[1] += two
        return carry

    lax.fori_loop(0, strip // 16, pool_body, 0)
    send_part(pooled_maps, slice(64, 96), ((0, HALO, SKIP_HALO + TOP_HALO),))
    empty = jnp.zeros((16, LANES), f32)
    one = acc[0]
    two = acc[1]
    stats = row_of(
        jnp.where(first, one, empty), jnp.where(first, empty, one),
        jnp.where(first, two, empty), jnp.where(first, empty, two),
        jnp.zeros((64, LANES), f32),
    )
    stats_out[...] = jnp.broadcast_to(stats, stats_out.shape)
    for store in stores:
        store.wait()


def crop_kernel(own_rows, strip_rows, style_columns, place, crop_rows, crop_group, meta, members,
                counts):
    crops = crop_rows.shape[0]
    rows = lanes_of((8, LANES)) + place[0] - HALO
    which = lax.broadcasted_iota(jnp.int32, (8, LANES), 0)
    start = jnp.int32(0)
    joined = jnp.zeros((8, LANES), jnp.int32)
    groups = jnp.full((8, LANES), -1, jnp.int32)
    pixels = jnp.zeros((8, LANES), jnp.int32)
    for k in range(crops):
        size = crop_rows[k]
        inside = jnp.logical_and(rows >= start, rows < start + size)
        linked = jnp.logical_and(rows > start, rows < start + size)
        joined = jnp.where(linked, 1, joined)
        groups = jnp.where(inside, crop_group[k], groups)
        pixels = pixels + jnp.where(which == crop_group[k], size * style_columns, 0)
        start = start + size
    meta[...] = jnp.where(which == 0, joined, groups)
    members[...] = (groups == which).astype(f32)
    counts[...] = jnp.maximum(pixels, 1).astype(f32)


def pack_kernel(enc_first, enc, dec, eskip, dskip, dense, in_gain, in_shift, enc_gain,
                enc_shift, dec_gain, dec_shift, out, small):
    taps = [enc[k, i, j] for k in range(3) for i in range(3) for j in range(3)]
    taps += [dec[k, i, j] for k in range(4) for i in range(3) for j in range(3)]
    taps.append(dskip[...])
    for k in range(32):
        pair = [tap.astype(f32) for tap in taps[2 * k : 2 * k + 2]]
        out[k] = jnp.concatenate(pair, axis=1).astype(bf16)
    quarters = [enc_first[i, j].astype(f32) for i in range(3) for j in range(3)]
    quarters.append(eskip[...].astype(f32))
    quarters += [jnp.zeros((32, 32), f32)] * 2
    for k in range(3):
        out[32 + k] = jnp.concatenate(quarters[4 * k : 4 * k + 4], axis=1).astype(bf16)
    for k in range(6):
        out[35 + k] = dense[k // 2, :, LANES * (k % 2) : LANES * (k % 2 + 1)]
    small[...] = jnp.zeros_like(small)
    at = 0
    for source in (in_gain, in_shift, enc_gain, enc_shift, dec_gain, dec_shift):
        count, width = source.shape
        small[at : at + count, :width] = source[...]
        at += count
    rest = small[...]
    for k in range(3):
        part = rest.astype(bf16)
        out[41 + k] = part
        rest = rest - part.astype(f32)


def style_sum_kernel(own_rows, core, style, members, out):
    start = pl.multiple_of(core[0] * own_rows, own_rows)
    total = style[0, pl.ds(start, own_rows), :].astype(f32)
    for column in range(1, style.shape[0]):
        total = total + style[column, pl.ds(start, own_rows), :].astype(f32)
    here = pltpu.roll(members[...], LANES - HALO, axis=1)[:, :own_rows]
    sums = jnp.dot(here, total, precision=lax.Precision.HIGHEST, preferred_element_type=f32)
    out[...] = jnp.concatenate([sums[j : j + 1] for j in range(GROUPS)], axis=1)


def join_kernel(own_rows, core, mine, pair, same, cross, skip, top, pooled):
    pair_rows = own_rows + HALO
    total = own_rows + 2 * HALO
    starts = (0, SKIP_HALO, SKIP_HALO + TOP_HALO)

    def put(rows, half, source):
        channels = slice(32 * half, 32 * (half + 1))
        narrow = slice(16 * half, 16 * (half + 1))
        here = slice(rows, rows + pair_rows)
        skip[here, channels] = source[:, :32]
        top[here, channels] = source[:, 32:64]
        pooled[here, narrow] = source[:, 64:80].astype(f32) + source[:, 80:96].astype(f32)

    def edge(above, half, source):
        channels = slice(32 * half, 32 * (half + 1))
        narrow = slice(16 * half, 16 * (half + 1))
        for out, count, start in ((skip, SKIP_HALO, starts[0]), (top, TOP_HALO, starts[1])):
            rows = HALO - count if above else pair_rows
            out[rows : rows + count, channels] = source[start : start + count]
            left = slice(0, rows) if above else slice(rows + count, total)
            out[left, channels] = jnp.zeros((HALO - count, 32, LANES), bf16)
        rows = 0 if above else pair_rows
        lines = source[starts[2] :].astype(f32)
        pooled[rows : rows + HALO, narrow] = lines[:, :16] + lines[:, 16:]

    @pl.when(core[0] == 0)
    def _():
        edge(True, 0, same)
        edge(True, 1, cross)
        put(HALO, 0, mine)
        put(HALO, 1, pair)

    @pl.when(core[0] == 1)
    def _():
        put(0, 0, pair)
        put(0, 1, mine)
        edge(False, 0, cross)
        edge(False, 1, same)


def gather_rows(kernel_out, perms):
    local, pair, same, cross = kernel_out
    return (
        local,
        lax.ppermute(pair, both, perms[0]),
        lax.ppermute(same, both, perms[1]),
        lax.ppermute(cross, both, perms[2]),
    )


CONVS = (
    ("first", 0), ("e0", 1), ("e1", 2), ("e2", 3), ("d0", 4), ("d1", 5), ("d2", 6), ("d3", 7)
)
NT = (((1,), (1,)), ((), ()))


def one_hot(height, width, offset):
    rows = lax.broadcasted_iota(jnp.int32, (height, width), 0)
    return (lanes_of((height, width)) == rows + offset).astype(f32).astype(bf16)


def piece_of(packed, which, index):
    if which in (0, 3):
        spot = 9 if which == 3 else 3 * index[0] + index[1]
        lane = 32 * (spot % 4)
        return packed[32 + spot // 4].astype(f32)[:, lane : lane + 32].astype(bf16)
    if which == 5:
        block = 35 + 2 * index[0]
        return jnp.concatenate([packed[block], packed[block + 1]], axis=1)
    spot = 63
    if which in (1, 2):
        spot = (0 if which == 1 else 27) + 9 * index[0] + 3 * index[1] + index[2]
    lane = 64 * (spot % 2)
    return packed[spot // 2].astype(f32)[:, lane : lane + 64].astype(bf16)


def prepare_kernel(core, stats, own, other, stats_copy, *refs):
    refs = list(refs)
    stats_copy[...] = stats[...]
    first = core[0] == 0
    mine, theirs = 32 * core[0], 32 * (1 - core[0])

    def whole(which, *index):
        left, right = piece_of(own, which, index), piece_of(other, which, index)
        return jnp.where(
            first,
            jnp.concatenate([left, right], axis=0),
            jnp.concatenate([right, left], axis=0),
        )

    def mixed(which, index, maker):
        return maker(piece_of(own, which, index), mine) + maker(
            piece_of(other, which, index), theirs
        )

    def put(width, lane):
        return lambda value, offset: dot(value, one_hot(32, width, lane + offset))

    rows_t = lax.broadcasted_iota(jnp.int32, (64, 32), 0)
    lanes_t = lanes_of((64, 32))

    def turn(value, offset):
        spot = (rows_t == lanes_t + offset).astype(f32).astype(bf16)
        return lax.dot_general(spot, value, NT, preferred_element_type=f32)

    ahead_all, back_all = refs.pop(0), refs.pop(0)
    ahead_all[...] = jnp.zeros_like(ahead_all)
    back_all[...] = jnp.zeros_like(back_all)
    back = back_all.at[0]
    for i in range(3):
        line = None
        span = None
        for j in range(3):
            term = mixed(0, (i, j), put(192, 64 * (2 - j)))
            line = term if line is None else line + term
            piece = dot(mixed(0, (i, j), turn).astype(bf16), one_hot(32, 96, 32 * j))
            span = piece if span is None else span + piece
        ahead_all[0, 64 * i : 64 * (i + 1), :96] = span.astype(bf16)
        back[32 * (2 - i) : 32 * (3 - i), :] = line.astype(bf16)
    eye = one_hot(64, 64, 0)
    empty = jnp.zeros((64, 64), bf16)
    for spot, (name, which, layer) in enumerate((
        ("e0", 1, 0), ("e1", 1, 1), ("e2", 1, 2),
        ("d0", 2, 0), ("d1", 2, 1), ("d2", 2, 2), ("d3", 2, 3),
    )):
        ahead, back = ahead_all.at[spot + 1], back_all.at[spot + 1]
        width = 256
        for i in range(3):
            taps = [whole(which, layer, i, j) for j in range(3)]
            span = None
            for j in range(3):
                piece = dot(taps[j], one_hot(64, width, 64 * j))
                span = piece if span is None else span + piece
            if i == 1 and name == "e0":
                turned = mixed(3, (Ellipsis,), turn).astype(bf16)
                span = span + dot(turned, one_hot(32, width, 192))
            if i == 1 and name == "d1":
                span = span + dot(whole(4, Ellipsis), one_hot(64, width, 192))
            ahead[64 * i : 64 * (i + 1), :] = span.astype(bf16)
            tall = jnp.concatenate([taps[2], taps[1], taps[0]], axis=0)
            back[64 * (2 - i) : 64 * (3 - i), :] = lax.dot_general(
                eye, tall, NT, preferred_element_type=f32
            ).astype(bf16)
        if name == "e0":
            back[192:224, :] = mixed(3, (Ellipsis,), put(192, 64)).astype(bf16)
        if name == "d1":
            tall = jnp.concatenate([empty, whole(4, Ellipsis), empty], axis=0)
            back[192:, :] = lax.dot_general(
                eye, tall, NT, preferred_element_type=f32
            ).astype(bf16)
    def small_of(packed):
        value = packed[41].astype(f32) + packed[42].astype(f32) + packed[43].astype(f32)
        tall = jnp.concatenate([value, jnp.zeros((LANES - 32, LANES), f32)], axis=0)
        return jnp.transpose(tall)

    flip_own, flip_other = small_of(own), small_of(other)

    def full(half):
        left, right = flip_own[:half], flip_other[:half]
        return jnp.where(
            first,
            jnp.concatenate([left, right], axis=0),
            jnp.concatenate([right, left], axis=0),
        )

    narrow, wide = full(16), full(32)
    small_norms, norms = refs.pop(0), refs.pop(0)
    for source, norm, gain, shift in (
        (narrow, small_norms.at[0], 0, 2), (narrow, small_norms.at[1], 1, 3),
        (wide, norms.at[0], 4, 7), (wide, norms.at[1], 5, 8), (wide, norms.at[2], 6, 9),
        (wide, norms.at[3], 10, 15), (wide, norms.at[4], 11, 16), (wide, norms.at[5], 12, 17),
        (wide, norms.at[6], 13, 18), (wide, norms.at[7], 14, 19),
    ):
        norm[0] = jnp.broadcast_to(source[:, gain : gain + 1], norm.shape[1:])
        norm[1] = jnp.broadcast_to(source[:, shift : shift + 1], norm.shape[1:])


def style_kernel(core, stats, counts, members, own, other, unit_out, *features):
    total = jnp.sum(stats[:, LANES:], axis=0, keepdims=True)
    channels = unit_out.shape[1]
    rows = lax.broadcasted_iota(jnp.int32, (8, channels), 0)
    sums = jnp.zeros((8, channels), f32)
    for j in range(GROUPS):
        piece = jnp.broadcast_to(total[:, channels * j : channels * (j + 1)], (8, channels))
        sums = sums + jnp.where(rows == j, piece, 0.0)
    means = sums / counts[:, :1]
    unit = means * lax.rsqrt(jnp.sum(means * means, axis=1, keepdims=True) + 1e-06)
    unit_out[...] = unit
    for layer, feature in enumerate(features):
        left = piece_of(own, 5, (layer,)).astype(f32)
        right = piece_of(other, 5, (layer,)).astype(f32)
        dense = jnp.where(
            core[0] == 0,
            jnp.concatenate([left, right], axis=0),
            jnp.concatenate([right, left], axis=0),
        )
        made = lax.dot_general(
            dense, unit, NT, precision=lax.Precision.HIGHEST, preferred_element_type=f32
        )
        out = jnp.zeros((64, LANES), f32)
        for j in range(GROUPS):
            out = out + made[:, j : j + 1] * members[j : j + 1, :]
        feature[...] = out


def input_grad_kernel(own_rows, inv_count, core, slope_a, slope_s, values, stats, sums, norms,
                      kept, sent):
    sums, norm_a, norm_s = [sums], norms.at[1], norms.at[0]
    center, scale = stats[0], stats[1]
    outer_s, col_s, const_s = back_columns(
        sums, 0, 32, 0, center, scale, norm_s[0], inv_count, 8
    )
    outer_a, col_a, const_a = back_columns(
        sums, 0, 32, 64, center, scale, norm_a[0], inv_count, 8
    )
    slope_col = col_s + col_a
    const_col = const_s + const_a
    first = core[0] == 0

    def body(step, carry):
        for k in range(4):
            row = 4 * step + k
            at = HALO + row
            grad = const_col - values[at] * slope_col
            grad = grad + slope_a[row + 2] * outer_a + slope_s[row + 2] * outer_s
            grad = (grad * 0.25).astype(bf16)
            low, high = grad[:16], grad[16:]
            kept[row] = jnp.where(first, low, high)
            sent[row] = jnp.where(first, high, low)
        return carry

    lax.fori_loop(0, own_rows // 4, body, 0)


def pixels_out_kernel(own_rows, core, kept, received, out, spread):
    home = pixel_home(lanes_of(spread.shape))
    rows = lax.broadcasted_iota(jnp.int32, spread.shape, 0)
    spread[...] = (home == rows).astype(f32).astype(bf16)
    wide = 4 * FULL_W
    half = own_rows // 2

    def body(step, carry):
        for which, source in enumerate((kept, received)):
            place = core[0] if which == 0 else 1 - core[0]
            left = jnp.concatenate(
                [
                    jnp.concatenate([source[8 * step + 2 * k], source[8 * step + 2 * k + 1]], axis=1)
                    for k in range(4)
                ],
                axis=0,
            )
            grown = dot(left, spread[...])
            for k in range(4):
                at = pl.multiple_of((place * half + 4 * step + k) * wide, LANES)
                out[:, pl.ds(at, wide)] = grown[16 * k : 16 * (k + 1)]
        return carry

    lax.fori_loop(0, own_rows // 8, body, 0)


def flat_kernel(own_rows, start, core, kept, received, out):
    lanes = lanes_of((32, LANES)).astype(f32).astype(bf16)

    def body(step, carry):
        for which, source in enumerate((kept, received)):
            place = core[0] if which == 0 else 1 - core[0]
            skip = 2 if which == 0 else start
            rows = [source[8 * step + k + skip] for k in range(8)]
            base = pl.multiple_of((place * own_rows + 8 * step) * POOL_W, LANES)
            for t in range(7):
                left = rows[t] if t == 0 else roll(rows[t], -16 * t)
                tile = jnp.where(
                    lanes < POOL_W - 16 * t, left, roll(rows[t + 1], POOL_W - 16 * t)
                )
                out[:, pl.ds(pl.multiple_of(base + LANES * t, LANES), LANES)] = tile.astype(f32)
        return carry

    lax.fori_loop(0, own_rows // 8, body, 0)


def pack_maps_kernel(own_rows, decoded, skip, out):
    def body(row, carry):
        out[row] = decoded[row + 2]
        out[own_rows + row] = skip[row + 2]
        return carry

    lax.fori_loop(0, own_rows, body, 0)


NAMES = ("d3", "d2", "d1", "d0", "e2", "e1", "e0", "first")
TILES = tuple((name, 0) for name in NAMES) + (
    ("d1", 1), ("e0", 1), ("d3", "d2"), ("d0", "e2"), ("e1", 1)
)
EXTRA = 16


def tile_of(parts, tile):
    name, which = tile
    if not isinstance(which, str):
        return parts[name][:, LANES * which : LANES * (which + 1)]
    left, right = parts[name][:, LANES:], parts[which][:, LANES:]
    return jnp.where(lanes_of(left.shape) < 64, left, pltpu.roll(right, 64, axis=1))


def split_two(value):
    upper = value.astype(bf16).astype(f32)
    return jnp.concatenate([upper, value - upper], axis=0).astype(bf16)


def sum_two(packed):
    value = packed.astype(f32)
    return value[:8] + value[8:]


def pack_grads_kernel(*refs):
    parts, stats, out = dict(zip(NAMES, refs[:-2])), refs[-2], refs[-1]
    for k, tile in enumerate(TILES):
        out[96 * k : 96 * (k + 1)] = tile_of(parts, tile).astype(bf16)
    out[96 * len(TILES) :] = split_two(stats[...])


def join_grads_kernel(per_strip, *refs):
    parts, stats, got, out = dict(zip(NAMES, refs[:-3])), refs[-3], refs[-2], refs[-1]
    chunk = per_strip + EXTRA
    strips = out.shape[0] // chunk
    at = 0
    for tile in TILES:
        value = (tile_of(parts, tile) + got[at : at + 96].astype(f32)).astype(bf16)
        for row in range(0, 96, 16):
            spot = at // per_strip * chunk + at % per_strip
            out[spot : spot + 16] = value[row : row + 16]
            at += 16
    lines = split_two(stats[...] + sum_two(got[at : at + 16]))
    for strip in range(strips):
        out[chunk * strip + per_strip : chunk * (strip + 1)] = lines
    while at < per_strip * strips:
        spot = at // per_strip * chunk + at % per_strip
        out[spot : spot + 16] = jnp.zeros((16, LANES), bf16)
        at += 16


def add_grads_kernel(per_strip, values, out, stats):
    chunk = per_strip + EXTRA
    strips = values.shape[0] // chunk
    total = values[:per_strip].astype(f32)
    lines = sum_two(values[per_strip:chunk])
    for k in range(1, strips):
        total = total + values[chunk * k : chunk * k + per_strip].astype(f32)
        lines = lines + sum_two(values[chunk * k + per_strip : chunk * (k + 1)])
    total = total.astype(bf16)
    stats[...] = lines
    for k in range(strips):
        out[per_strip * k : per_strip * (k + 1)] = total


def finish_kernel(seen, core, grads, unit, sp, sh0, se1, sh2, se2, *refs):
    refs = list(refs)
    su1, su2, su3 = [take(refs, count) for count in seen]
    (first_out, enc_out, eskip_out, in_gain, in_shift, enc_gain, enc_shift, dec_out, dskip_out,
     dec_gain, dec_shift, dense_out) = refs
    sp, sh0, se1, sh2, se2 = [sp], [sh0], [se1], [sh2], [se2]
    places = {}
    for k, (name, which) in enumerate(TILES):
        if isinstance(which, str):
            places[name, 1] = (k, 0)
            places[which, 1] = (k, 64)
        else:
            places[name, which] = (k, 0)

    def block(name, which):
        spot, lane = places[name, which]
        return grads[96 * spot : 96 * (spot + 1)].astype(f32), lane

    for refs, names in ((enc_out, ("e0", "e1", "e2")), (dec_out, ("d0", "d1", "d2", "d3"))):
        for k, name in enumerate(names):
            for i in range(3):
                source, lane = block(name, i // 2)
                lane = lane + 64 * (i % 2)
                for j in range(3):
                    refs[k, i, j] = source[32 * j : 32 * (j + 1), lane : lane + 64]
    tall = block("first", 0)[0]
    flipped = jnp.transpose(jnp.concatenate([tall, tall[:32]], axis=0))
    for j in range(3):
        for i in range(3):
            first_out[i, j] = flipped[32 * i : 32 * (i + 1), 32 * j : 32 * (j + 1)]
    tall = block("e0", 1)[0]
    flipped = jnp.transpose(jnp.concatenate([tall, tall[:32]], axis=0))
    eskip_out[...] = flipped[64:96, 32:64]
    dskip_out[...] = block("d1", 1)[0][32:64, 64:128]
    lines = [total_of(sp, 1 + k, 8) for k in range(6)]
    rows = lax.broadcasted_iota(jnp.int32, (LANES, LANES), 0)
    tall = jnp.zeros((LANES, LANES), f32)
    for k, line in enumerate(lines):
        tall = jnp.where(rows == k, jnp.broadcast_to(line, (LANES, LANES)), tall)
    flipped = jnp.transpose(tall)
    for layer in range(3):
        out = jnp.zeros((32, unit.shape[1]), f32)
        for j in range(GROUPS):
            at = 64 * (j % 2)
            column = slice(2 * layer + j // 2, 2 * layer + j // 2 + 1)
            picked = jnp.where(
                core[0] == 0, flipped[at : at + 32, column], flipped[at + 32 : at + 64, column]
            )
            out = out + picked * unit[j : j + 1, :]
        dense_out[layer] = out

    def pick(stats, slot, lane, half, period=1):
        total = total_of(stats, slot, period)
        low = total[:1, lane : lane + half]
        high = total[:1, lane + half : lane + 2 * half]
        return jnp.where(core[0] == 0, low, high)

    for k in range(2):
        in_shift[k : k + 1, :] = pick(sp, 0, 64 * k, 16, 8)
        in_gain[k : k + 1, :] = pick(sp, 0, 64 * k + 32, 16, 8)
    for k, stats in enumerate((sh0, se1, sh2)):
        enc_shift[k : k + 1, :] = pick(stats, 0, 0, 32)
        enc_gain[k : k + 1, :] = pick(stats, 0, 64, 32)
    for k, (stats, slot) in enumerate(((se2, 0), (se2, 1), (su1, 0), (su2, 0), (su3, 0))):
        dec_shift[k : k + 1, :] = pick(stats, slot, 0, 32, 2 if stats is se2 else 1)
        dec_gain[k : k + 1, :] = pick(stats, slot, 64, 32, 2 if stats is se2 else 1)


def pixel_home(index):
    upper = (index >= 2 * FULL_W).astype(jnp.int32)
    line = index - 2 * FULL_W * upper
    column = line - FULL_W * (line >= FULL_W).astype(jnp.int32)
    return LANES * upper + column // 2


def share(values):
    return (lax.all_to_all(values, both, 0, 0, tiled=True),)


def per_device(
    pixels, skip_map, style_map, crop_rows, crop_group, enc_first, enc_convs, enc_skip,
    enc_in_gain, enc_in_shift, enc_gain, enc_shift, dec_convs, dec_skip, dec_gain, dec_shift,
    dense, out_grad,
):
    strip_rows = skip_map.shape[1] // POOL_W
    own = strip_rows // 2
    strips = lax.axis_size("rows")
    devices = 2 * strips
    inv_count = 1.0 / (strips * strip_rows * POOL_W)
    core_index = lax.axis_index("ch").astype(jnp.int32)
    core = core_index[None]
    total = own + 2 * HALO
    place = (lax.axis_index("rows").astype(jnp.int32) * strip_rows + core_index * own)[None]
    swap = [(i, i ^ 1) for i in range(devices)]
    same = []
    cross = []
    for i in range(strips - 1):
        same += [(2 * i, 2 * i + 2), (2 * i + 3, 2 * i + 1)]
        cross += [(2 * i + 1, 2 * i + 2), (2 * i + 2, 2 * i + 1)]
    perms = (swap, same, cross)
    pair_rows = own + HALO

    def turned(value):
        return jnp.swapaxes(value, -1, -2)

    packed, _ = call(
        pack_kernel, "pack",
        [(value, False) for value in
         (enc_first, turned(enc_convs), turned(dec_convs), enc_skip, turned(dec_skip),
          turned(dense), enc_in_gain, enc_in_shift, enc_gain, enc_shift, dec_gain, dec_shift)],
        [((44, 32, LANES), bf16), ((32, LANES), f32)], cost=1,
    )
    packed_other = lax.ppermute(packed, both, swap)
    *made, stats_p = call(
        functools.partial(entry_kernel, own), "entry",
        [(core, True), (skip_map, "hbm"), (out_grad, "hbm"), (pixels, "hbm")],
        [
            ((pair_rows, 96, LANES), bf16, "hbm"), ((pair_rows, 96, LANES), bf16, "hbm"),
            ((SKIP_HALO + TOP_HALO + HALO, 32, LANES), bf16, "hbm"),
            ((SKIP_HALO + TOP_HALO + HALO, 32, LANES), bf16, "hbm"), ((devices, LANES), f32),
        ],
        [pltpu.VMEM((2, 16, LANES), f32)]
        + [pltpu.VMEM(value.shape, bf16) for value in (skip_map, out_grad, pixels)]
        + [pltpu.VMEM((4 * FULL_W, 2 * LANES), bf16), pltpu.VMEM((strip_rows, 64, LANES), bf16)]
        + [pltpu.VMEM((strip_rows, 32, LANES), bf16)]
        + [pltpu.SemaphoreType.DMA((3,)), pltpu.SemaphoreType.DMA((10,))],
        limit=60,
    )
    map_parts = gather_rows(made, perms)
    meta, members, counts = call(
        functools.partial(crop_kernel, own, strip_rows, style_map.shape[1]), "crops",
        [(place, True), (crop_rows, True), (crop_group, True)],
        [((8, LANES), jnp.int32), ((8, LANES), f32), ((8, LANES), f32)], cost=1,
    )
    (style_sums,) = call(
        functools.partial(style_sum_kernel, own), "style_sums",
        [(core, True), (jnp.swapaxes(style_map, 0, 1), False), (members, False)],
        [((1, GROUPS * style_map.shape[2]), f32)], cost=1,
    )
    stats_p, ahead, back, norms_in, norms = call(
        prepare_kernel, "prepare",
        [(core, True), (stats_p, False), (packed, False), (packed_other, False)],
        [
            ((devices, LANES), f32),
            ((8, 192, 256), bf16), ((8, 256, 192), bf16),
            ((2, 2, 32, LANES), f32), ((8, 2, 64, LANES), f32),
        ],
        after=(style_sums,),
    )
    stats_p = share(stats_p)
    skip_full, top_full, pooled = call(
        functools.partial(join_kernel, own), "join",
        [(core, True)] + [(part, False) for part in map_parts],
        [((total, 64, LANES), bf16), ((total, 64, LANES), bf16), ((total, 32, LANES), f32)],
        after=stats_p,
    )

    go = functools.partial(
        forward, keep=meta, norms=norms, weights=ahead, own_rows=own, inv_count=inv_count,
        out_rows=devices,
    )
    h0, a0, s0, c_p, t_h0 = go(
        "ahead_h0", values=pooled, stats=stats_p, norms=norms_in, spots=(1, 0), layer=0, f=13,
        after=(top_full,),
    )
    t_h0 = share(t_h0)
    e1, a1, c_h0, t_e1 = go(
        "ahead_e1", values=h0, stats=t_h0, spots=(0,), layer=1, f=12, skip_in=s0,
        payload=style_sums,
    )
    t_e1 = share(t_e1)
    unit, *feature = call(
        style_kernel, "style",
        [(core, True), (t_e1[0], False), (counts, False), (members, False), (packed, False),
         (packed_other, False)],
        [((8, style_map.shape[2]), f32)] + [((64, LANES), f32)] * 3, cost=1,
    )
    h2, a2, c_e1, t_h2 = go(
        "ahead_h2", values=e1, stats=t_e1, spots=(1,), layer=2, f=11, after=(unit,)
    )
    t_h2 = share(t_h2)
    e2, a3, c_h2, t_e2 = go(
        "ahead_e2", values=h2, stats=t_h2, spots=(2,), layer=3, f=10, residual=e1
    )
    t_e2 = share(t_e2)
    u1, b0, q0, c_e2, t_u1 = go(
        "ahead_u1", values=e2, stats=t_e2, spots=(4, 3), layer=4, f=9, skip_map=skip_full,
        feature=feature[0],
    )
    t_u1 = share(t_u1)
    u2, raw_d1, b1, c_u1, t_u2 = go(
        "ahead_u2", values=u1, stats=t_u1, spots=(5,), layer=5, f=8, skip_in=q0,
        skip_map=skip_full, feature=feature[1], keep_raw=True,
    )
    t_u2 = share(t_u2)
    u3, b2, c_u2, t_u3 = go(
        "ahead_u3", values=u2, stats=t_u2, spots=(6,), layer=6, f=7, feature=feature[2]
    )
    t_u3 = share(t_u3)
    ret = functools.partial(
        backward, keep=meta, core=core, norms=norms, below_norms=norms, weights=back,
        own_rows=own, inv_count=inv_count, out_rows=devices,
    )
    parts = {}
    slope_u3, s_u3, *parts["d3"], sums_top, b3, c_u3 = ret(
        "back_top", slopes=[], values=None, stats=None, sums=(), spots=(), layer=7, below=u3,
        below_stats=t_u3[0], below_spot=7, act=None, b=8, extra=top_full, export=True,
    )
    s_u3 = share(s_u3)
    slope_u2, s_u2, *parts["d2"], sums_u3 = ret(
        "back_u3", slopes=[slope_u3], values=u3, stats=c_u3, sums=s_u3, spots=(7,), layer=6,
        below=u2, below_stats=c_u2, below_spot=6, act=b2, b=7, export=True,
    )
    s_u2 = share(s_u2)
    pure_u2, slope_u1, slope_q0, s_u1, *parts["d1"], sums_d1 = ret(
        "back_u2", slopes=[slope_u2], values=u2, stats=c_u2, sums=s_u2, spots=(6,), layer=5,
        below=u1, below_stats=c_u1, below_spot=5, act=b1, b=6, extra=top_full, extra_rows=64,
        save="own", skip_in=q0, export=True,
    )
    s_u1 = share(s_u1)
    slope_b0, skip_kept, skip_sent, s_e2, *parts["d0"], sums_u1 = ret(
        "back_u1", slopes=[slope_u1], values=u1, stats=c_u1, sums=s_u1, spots=(5,), layer=4,
        below=e2, below_stats=c_e2, below_spot=4, act=b0, b=5, below_side=slope_q0,
        other=pure_u2, export=True,
    )
    s_e2 = share(s_e2)
    pure_e2, slope_h2, s_h2, *parts["e2"] = ret(
        "back_e2", slopes=[slope_q0, slope_b0], values=e2, stats=c_e2, sums=s_e2, spots=(3, 4),
        layer=3, below=h2, below_stats=c_h2, below_spot=2, act=a3, b=4, save="all",
    )
    s_h2 = share(s_h2)
    slope_e1, s_e1, *parts["e1"] = ret(
        "back_h2", slopes=[slope_h2], values=h2, stats=c_h2, sums=s_h2, spots=(2,), layer=2,
        below=e1, below_stats=c_e1, below_spot=1, act=a2, b=3,
    )
    s_e1 = share(s_e1)
    slope_h0, slope_s0, s_h0, *parts["e0"] = ret(
        "back_e1", slopes=[slope_e1], values=e1, stats=c_e1, sums=s_e1, spots=(1,), layer=1,
        below=h0, below_stats=c_h0, below_spot=0, act=a1, b=2, extra=pure_e2, extra_rows=32,
        skip_in=s0,
    )
    s_h0 = share(s_h0)
    slope_a0, s_p, *parts["first"] = ret(
        "back_h0", slopes=[slope_h0], values=h0, stats=c_h0, sums=s_h0, spots=(0,), layer=0,
        below=pooled, below_stats=c_p, below_norms=norms_in, below_spot=1, act=a0, b=1,
        below_side=slope_s0, gathered=(sums_top, sums_u3, sums_d1, sums_u1),
    )
    tall = 96 * len(TILES)
    per_strip = -(-tall // (16 * strips)) * 16
    (sent,) = call(
        pack_grads_kernel, "pack_grads",
        [(parts[name][1], False) for name in NAMES] + [(s_p, False)],
        [((tall + EXTRA, LANES), bf16)], cost=1,
    )
    got = lax.ppermute(sent, both, swap)
    (joined,) = call(
        functools.partial(join_grads_kernel, per_strip), "join_grads",
        [(parts[name][0], False) for name in NAMES] + [(s_p, False), (got, False)],
        [(((per_strip + EXTRA) * strips, LANES), bf16)], cost=1,
    )
    scattered = lax.all_to_all(joined, "rows", 0, 0, tiled=True)
    decoded_kept, decoded_sent = call(
        functools.partial(decode_kernel, own), "decode",
        [(meta, True), (core, True), (b3, False), (ahead, False), (raw_d1, False)],
        [((own + 4, 32, LANES), bf16), ((own + 4, 32, LANES), bf16)],
        [pltpu.VMEM((2, 64, LANES), f32)], after=(s_p,),
    )
    (maps_sent,) = call(
        functools.partial(pack_maps_kernel, own), "pack_maps",
        [(decoded_sent, False), (skip_sent, False)],
        [((2 * own, 32, LANES), bf16)], cost=0.1,
    )
    maps_got = lax.ppermute(maps_sent, both, swap)
    (skip_grad,) = call(
        functools.partial(flat_kernel, own, own), "flat_skip",
        [(core, True), (skip_kept, False), (maps_got, False)],
        [((32, strip_rows * POOL_W), f32)], limit=60, cost=0.2,
    )
    (decoded,) = call(
        functools.partial(flat_kernel, own, 0), "flat_decoded",
        [(core, True), (decoded_kept, False), (maps_got, False)],
        [((32, strip_rows * POOL_W), f32)], limit=60, cost=0.2,
    )
    added, s_p = call(
        functools.partial(add_grads_kernel, per_strip), "add_grads", [(scattered, False)],
        [((per_strip * strips, LANES), bf16), ((8, LANES), f32)], limit=60, cost=1,
        after=(skip_grad, decoded),
    )
    grads = lax.all_to_all(added, "rows", 0, 0, tiled=True)
    pix_kept, pix_sent = call(
        functools.partial(input_grad_kernel, own, inv_count), "back_pooled",
        [(core, True), (slope_a0, False), (slope_s0, False), (pooled, False),
         (c_p, False), (s_p, False), (norms_in, False)],
        [((own, 16, LANES), bf16), ((own, 16, LANES), bf16)], cost=1,
    )
    pix_got = lax.ppermute(pix_sent, both, swap)
    (pixels_grad,) = call(
        functools.partial(pixels_out_kernel, own), "pixels_out",
        [(core, True), (pix_kept, False), (pix_got, False)],
        [((16, 4 * strip_rows * POOL_W), f32)],
        [pltpu.VMEM((2 * LANES, 4 * FULL_W), bf16)], limit=10, cost=0.5,
    )
    outs = [
        ((3, 3, 32, 32), f32), ((3, 3, 3, 32, 64), f32), ((32, 32), f32), ((2, 16), f32),
        ((2, 16), f32), ((3, 32), f32), ((3, 32), f32), ((4, 3, 3, 32, 64), f32), ((32, 64), f32),
        ((5, 32), f32), ((5, 32), f32), ((3, 32, style_map.shape[2]), f32),
    ]
    (s_h0,), (s_e1,), (s_h2,), (s_e2,) = s_h0, s_e1, s_h2, s_e2
    rest = call(
        functools.partial(finish_kernel, (len(s_u1), len(s_u2), len(s_u3))), "finish",
        [(core, True), (grads, False)]
        + [(value, False)
           for value in (unit, s_p, s_h0, s_e1, s_h2, s_e2, *s_u1, *s_u2, *s_u3)],
        outs, limit=8,
    )
    rest = list(rest)
    for spot in (1, 7, 8, 11):
        rest[spot] = turned(rest[spot])
    return (decoded, pixels_grad, skip_grad) + tuple(rest)


def solution(mesh):
    placed = (
        P("ch", "rows"),
        P("ch", "rows"),
        P("rows", None, None),
        P(),
        P(),
        P(None, None, None, "ch"),
        P(None, None, None, None, "ch"),
        P(None, "ch"),
        P(None, "ch"),
        P(None, "ch"),
        P(None, "ch"),
        P(None, "ch"),
        P(None, None, None, None, "ch"),
        P(None, "ch"),
        P(None, "ch"),
        P(None, "ch"),
        P(None, None, "ch"),
        P("ch", "rows"),
    )
    return jax.shard_map(
        per_device,
        mesh=mesh,
        in_specs=placed,
        out_specs=(
            P("ch", "rows"),
            P("ch", "rows"),
            P("ch", "rows"),
            P(None, None, None, "ch"),
            P(None, None, None, None, "ch"),
            P(None, "ch"),
            P(None, "ch"),
            P(None, "ch"),
            P(None, "ch"),
            P(None, "ch"),
            P(None, None, None, None, "ch"),
            P(None, "ch"),
            P(None, "ch"),
            P(None, "ch"),
            P(None, None, "ch"),
        ),
        check_vma=False,
    )
```
